32 devices in a mesh: grp: 2 (over y), doc: 4 (over z), feat: 4 (over x, core).
Axes of the slice: x: 2, y: 2, z: 4, core: 2. Of those that a mesh axis runs over, the one named last changes fastest.
Arguments:
- matrix: float32 [4096, 16384], P(('grp', 'doc'), 'feat'), parts along dimension 0, may hold values from 10 to 8000
- doc_factor: float32 [4096, 256], P(('grp', 'doc')), parts along dimension 0, may hold values from 0.25 to 10
- feat_factor: float32 [512, 16384], P(('grp', 'doc'), 'feat'), parts along dimension 0, may hold values from 0.25 to 2.5
Outputs:
- new_doc: float32 [4096, 256], P(('grp', 'doc')), parts along dimension 0
- new_feat: float32 [512, 16384], P(('grp', 'doc'), 'feat'), parts along dimension 0
The draws below stay inside these ranges and needn't reach their ends.
There are 2 independent parts, one for each index of `grp`. The reference program is written for one: setup_inputs(seed, part) draws one part's arguments, and reference() takes and returns one part's arrays. A program takes and returns all parts, laid end to end along the dimension named above; each array names one. Nothing has to cross between parts.
All inputs are finite; a program needn't handle non-finite values.
Results may differ from the reference program's by a relative error of at most 0.0001.
Values sent between devices are 32-bit elements; how exact they have to be, the bound alone decides.
No kernel may reach another device: no remote copies, remote signals or barrier semaphores. Data moves between devices by JAX's collectives and lax.ppermute only.
A program may use at most 128 MiB of HBM per device.

```python
import math
import jax
import jax.numpy as jnp
from jax import lax

FEATURES = 16384
RANK = 256
INNER = 2
OUTER = 1
DOCS = 2048


def cluster_labels(key):
    labels_key = jax.random.fold_in(key, 7)
    shift_key, feature_key, component_key = jax.random.split(labels_key, 3)
    shift = jax.random.randint(shift_key, (), 0, 4)
    doc_label = (jnp.arange(DOCS, dtype=jnp.int32) * 4 // DOCS + shift) % 4
    feature_label = jax.random.randint(feature_key, (FEATURES,), 0, 4)
    component_label = jax.random.randint(component_key, (RANK,), 0, 4)
    return (doc_label, feature_label, component_label)


def draw_matrix(key, part):
    doc_label, feature_label, component_label = cluster_labels(key)
    value_key = jax.random.fold_in(key, 11)
    unit = jax.random.uniform(value_key, (DOCS, FEATURES), jnp.float32)
    base = 10.0 * jnp.exp(unit * jnp.log(100.0))
    matched = doc_label[:, None] == feature_label[None, :]
    return (base * jnp.where(matched, 8.0, 1.0)).astype(jnp.float32)


def draw_doc_factor(key, part):
    doc_label, feature_label, component_label = cluster_labels(key)
    value_key = jax.random.fold_in(key, 13)
    unit = jax.random.uniform(value_key, (DOCS, RANK), jnp.float32)
    base = 0.25 * jnp.exp(unit * jnp.log(10.0))
    matched = doc_label[:, None] == component_label[None, :]
    return (base * jnp.where(matched, 4.0, 1.0)).astype(jnp.float32)


def levels(stream_key, dims, shards, least, top_value):
    def one(position, parts):
        steps = jax.random.uniform(jax.random.fold_in(jax.random.fold_in(stream_key, 6), position), (parts,), jnp.float32, least / len(shards), top_value / len(shards))
        return jnp.repeat(jnp.exp(steps), dims[position] // parts).reshape((-1,) + (1,) * (len(dims) - position - 1))

    factor_of = one(*shards[0])
    for cut in shards[1:]:
        factor_of = factor_of * one(*cut)
    return factor_of


def setup_inputs(seed: int = 0, part: int = 0) -> dict:
    seeds = jax.random.split(jax.random.key(seed), 4)
    part_keys = jax.random.split(jax.random.fold_in(seeds[3], part), 4)
    return {
        "matrix": draw_matrix(jax.random.fold_in(jax.random.fold_in(seeds[3], part), 71), part),
        "doc_factor": draw_doc_factor(jax.random.fold_in(jax.random.fold_in(seeds[3], part), 71), part),
        "feat_factor": jnp.clip(jnp.exp(math.log(2.5) - 2.3025851 * jax.random.uniform(part_keys[2], (RANK, FEATURES), jnp.float32) ** levels(part_keys[2], (RANK, FEATURES), ((0, 4), (1, 4)), -0.2, 0.2)), 0.25, 2.5),
    }


highest = lax.Precision.HIGHEST


def reference(matrix, doc_factor, feat_factor):
    wmat = doc_factor
    hmat = feat_factor
    for outer_step in range(OUTER):
        colsum = jnp.sum(wmat, axis=0)
        for inner_step in range(INNER):
            product = jnp.dot(wmat, hmat, precision=highest, preferred_element_type=jnp.float32)
            ratio = matrix / product
            numerator = jnp.dot(wmat.T, ratio, precision=highest, preferred_element_type=jnp.float32)
            hmat = hmat * numerator / colsum[:, None]
        product = jnp.dot(wmat, hmat, precision=highest, preferred_element_type=jnp.float32)
        ratio = matrix / product
        wnumer = jnp.dot(ratio, hmat.T, precision=highest, preferred_element_type=jnp.float32)
        rowsum = jnp.sum(hmat, axis=1)
        wmat = wmat * wnumer / rowsum[None, :]
    return wmat, hmat
```

```python
import functools

import jax
import jax.numpy as jnp
from jax import lax
from jax.experimental import pallas as pl
from jax.experimental.pallas import tpu as pltpu
from jax.sharding import PartitionSpec as P

INNER = 2
WIDTH = 256
PAD = 8
VMEM = 48 * 1024 * 1024
NT = (((1,), (1,)), ((), ()))


def xor_pairs(count, mask):
    return [(i, i ^ mask) for i in range(count)]


def split(value):
    high = value.astype(jnp.bfloat16)
    low = (value - high.astype(jnp.float32)).astype(jnp.bfloat16)
    return high, low


def dot(left, right):
    return jnp.dot(left, right, preferred_element_type=jnp.float32)


def dot3(left, right):
    return dot(left[0], right[0]) + (dot(left[0], right[1]) + dot(left[1], right[0]))


def dot_nt(left, right):
    return lax.dot_general(left, right, NT, preferred_element_type=jnp.float32)


def prepare_kernel(blocks, *refs):
    w_refs, (high_ref, low_ref, high_t_ref, low_t_ref, sum_ref) = refs[:blocks], refs[blocks:]
    rows = w_refs[0].shape[0]
    total = jnp.zeros(sum_ref.shape, jnp.float32)
    for b in range(blocks):
        value = w_refs[b][...]
        high, low = split(value)
        high_ref[b * rows : (b + 1) * rows, :] = high
        low_ref[b * rows : (b + 1) * rows, :] = low
        turned = value.T
        high, low = split(turned)
        high_t_ref[:, b * rows : (b + 1) * rows] = high
        low_t_ref[:, b * rows : (b + 1) * rows] = low
        total = total + jnp.sum(turned, axis=1, keepdims=True)
    sum_ref[...] = total


def prepare(w_blocks):
    blocks = len(w_blocks)
    rows, rank = w_blocks[0].shape
    docs = blocks * rows
    half = jnp.bfloat16
    shapes = [
        jax.ShapeDtypeStruct((docs, rank), half),
        jax.ShapeDtypeStruct((docs, rank), half),
        jax.ShapeDtypeStruct((rank, docs), half),
        jax.ShapeDtypeStruct((rank, docs), half),
        jax.ShapeDtypeStruct((rank, 1), jnp.float32),
    ]
    return pl.pallas_call(
        functools.partial(prepare_kernel, blocks),
        out_shape=shapes,
        in_specs=[pl.BlockSpec(memory_space=pltpu.VMEM)] * blocks,
        out_specs=[pl.BlockSpec(memory_space=pltpu.VMEM)] * len(shapes),
        compiler_params=pltpu.CompilerParams(vmem_limit_bytes=VMEM),
        cost_estimate=pl.CostEstimate(flops=0, bytes_accessed=docs * rank * 12, transcendentals=0),
        name="prepare_w",
    )(*w_blocks)


def piece_kernel(blocks, parts, first, *refs):
    m_refs = refs[:blocks]
    high_ref, low_ref, high_t_ref, low_t_ref, sum_ref, h_ref = refs[blocks : blocks + 6]
    rest = refs[blocks + 6 :]
    wn_in = None if first else rest[0]
    h_out, wn_out = rest[0 if first else 1 :]
    rows = m_refs[0].shape[0]
    width = h_ref.shape[1]
    part_rows = rows // parts

    def ratio(b, factor):
        near = slice(b * rows, (b + 1) * rows)
        product = dot3((high_ref[near, :], low_ref[near, :]), factor)
        return split(m_refs[b][...] / product)

    factor = h_ref[...]
    for _ in range(INNER):
        pair = split(factor)
        total = None
        for b in range(blocks):
            near = slice(b * rows, (b + 1) * rows)
            term = dot3((high_t_ref[:, near], low_t_ref[:, near]), ratio(b, pair))
            total = term if total is None else total + term
        factor = factor * total / sum_ref[...]
    h_out[...] = factor
    pair = split(factor)
    ones = jnp.ones((PAD, width), jnp.bfloat16)
    row_sum = dot_nt(ones, pair[0]) + dot_nt(ones, pair[1])
    for b in range(blocks):
        high, low = ratio(b, pair)
        term = dot_nt(high, pair[0]) + (dot_nt(high, pair[1]) + dot_nt(low, pair[0]))
        for q in range(parts):
            body_rows = term[q * part_rows : (q + 1) * part_rows, :]
            if first:
                wn_out[b, q, :part_rows, :] = body_rows
                wn_out[b, q, part_rows:, :] = row_sum
            else:
                wn_out[b, q, :part_rows, :] = wn_in[b, q, :part_rows, :] + body_rows
                wn_out[b, q, part_rows:, :] = wn_in[b, q, part_rows:, :] + row_sum


def update_piece(m_blocks, weights, factor, sums, parts):
    blocks = len(m_blocks)
    rows, width = m_blocks[0].shape
    rank = factor.shape[0]
    first = sums is None
    sums_shape = (blocks, parts, rows // parts + PAD, rank)
    given = [*m_blocks, *weights, factor] + ([] if first else [sums])
    space = pl.BlockSpec(memory_space=pltpu.VMEM)
    return pl.pallas_call(
        functools.partial(piece_kernel, blocks, parts, first),
        out_shape=[
            jax.ShapeDtypeStruct((rank, width), jnp.float32),
            jax.ShapeDtypeStruct(sums_shape, jnp.float32),
        ],
        in_specs=[space] * len(given),
        out_specs=[space] * 2,
        input_output_aliases={} if first else {len(given) - 1: 1},
        compiler_params=pltpu.CompilerParams(vmem_limit_bytes=VMEM),
        cost_estimate=pl.CostEstimate(
            flops=30 * blocks * rows * width * rank,
            bytes_accessed=blocks * rows * (4 * width + 16 * rank),
            transcendentals=0,
        ),
        name="update_piece",
    )(*given)


def update_plain(m_blocks, w_blocks, factor, parts):
    highest = lax.Precision.HIGHEST
    whole_w = jnp.concatenate(w_blocks, axis=0)
    whole_m = jnp.concatenate(m_blocks, axis=0)
    blocks = len(m_blocks)
    rows, rank = w_blocks[0].shape
    column = jnp.sum(whole_w, axis=0)[:, None]
    for _ in range(INNER):
        ratio = whole_m / jnp.dot(whole_w, factor, precision=highest)
        numer = lax.dot_general(whole_w, ratio, (((0,), (0,)), ((), ())), precision=highest)
        factor = factor * numer / column
    ratio = whole_m / jnp.dot(whole_w, factor, precision=highest)
    wnumer = lax.dot_general(ratio, factor, NT, precision=highest)
    wnumer = wnumer.reshape(blocks, parts, rows // parts, rank)
    row_sum = jnp.broadcast_to(jnp.sum(factor, axis=1), (blocks, parts, PAD, rank))
    return factor, jnp.concatenate([wnumer, row_sum], axis=2)


def gather_feat(value, bits, feat, lead):
    for j in reversed(range(bits)):
        other = lax.ppermute(value, "feat", xor_pairs(1 << bits, 1 << j))
        axis = lead + bits - 1 - j
        low_side = (feat >> j) & 1 == 0
        value = jnp.where(
            low_side, jnp.stack([value, other], axis), jnp.stack([other, value], axis)
        )
    shape = value.shape
    return value.reshape(shape[:lead] + (-1,) + shape[-1:])


def scatter_feat(value, bits, feat):
    blocks = value.shape[0]
    value = value.reshape((blocks,) + (2,) * bits + value.shape[2:])
    for j in range(bits):
        bit = (feat >> j) & 1
        axis = bits - j
        kept = lax.dynamic_index_in_dim(value, bit, axis, keepdims=False)
        sent = lax.dynamic_index_in_dim(value, 1 - bit, axis, keepdims=False)
        value = kept + lax.ppermute(sent, "feat", xor_pairs(1 << bits, 1 << j))
    return value


def body(n_doc, n_feat, matrix, doc_factor, feat_factor):
    doc, feat = lax.axis_index("doc"), lax.axis_index("feat")
    bits = n_feat.bit_length() - 1
    rows, columns = matrix.shape
    share, rank = feat_factor.shape[0], doc_factor.shape[1]
    owned = columns // n_doc
    width = WIDTH if owned % WIDTH == 0 else owned
    pieces = owned // width
    part_rows = rows // n_feat

    def send(value, k):
        return lax.ppermute(value, "doc", xor_pairs(n_doc, k)) if k else value

    def m_piece(p):
        return [
            send(lax.dynamic_slice(matrix, (0, (doc ^ k) * owned + p * width), (rows, width)), k)
            for k in range(n_doc)
        ]

    w_part = lax.dynamic_slice_in_dim(doc_factor, feat * part_rows, part_rows, 0)
    w_parts = [send(w_part, k) for k in range(1, n_doc)]
    h_blocks = [
        send(lax.dynamic_slice(feat_factor, (0, (doc ^ k) * owned), (share, owned)), k)
        for k in range(n_doc)
    ]
    m_pieces = [m_piece(p) for p in range(pieces)]

    w_others = gather_feat(jnp.stack(w_parts), bits, feat, 1)
    w_blocks = [doc_factor] + [w_others[k] for k in range(n_doc - 1)]
    factor = jnp.zeros((rank, owned), jnp.float32)
    for k in range(n_doc):
        factor = lax.dynamic_update_slice(factor, h_blocks[k], ((doc ^ k) * share, 0))

    in_kernel = n_doc * rows * rank * 32 < VMEM
    if in_kernel:
        weights = prepare(w_blocks)
    new_feat = jnp.zeros((share, columns), jnp.float32)
    sums = None
    for p in range(pieces):
        h_piece = factor[:, p * width : (p + 1) * width]
        if in_kernel:
            h_new, sums = update_piece(m_pieces[p], weights, h_piece, sums, n_feat)
        else:
            h_new, more = update_plain(m_pieces[p], w_blocks, h_piece, n_feat)
            sums = more if sums is None else sums + more
        for k in range(n_doc):
            back = lax.dynamic_slice(h_new, ((doc ^ k) * share, 0), (share, width))
            new_feat = lax.dynamic_update_slice(
                new_feat, send(back, k), (0, (doc ^ k) * owned + p * width)
            )

    sums = scatter_feat(sums, bits, feat)
    total = sums[0]
    for k in range(1, n_doc):
        total = total + send(sums[k], k)
    new_part = w_part * total[:part_rows] / total[part_rows]
    new_doc = gather_feat(new_part, bits, feat, 0)
    return new_doc, new_feat


def solution(mesh):
    placed = (P(("grp", "doc"), "feat"), P(("grp", "doc"), None), P(("grp", "doc"), "feat"))
    return jax.shard_map(
        functools.partial(body, mesh.shape["doc"], mesh.shape["feat"]),
        mesh=mesh,
        in_specs=placed,
        out_specs=(P(("grp", "doc"), None), P(("grp", "doc"), "feat")),
        check_vma=False,
    )
```

```python
import functools

import jax
import jax.numpy as jnp
from jax import lax
from jax.experimental import pallas as pl
from jax.experimental.pallas import tpu as pltpu
from jax.sharding import PartitionSpec as P

INNER = 2
WIDTH = 256
PAD = 8
VMEM = 48 * 1024 * 1024
NT = (((1,), (1,)), ((), ()))


def xor_pairs(count, mask):
    return [(i, i ^ mask) for i in range(count)]


def split(value):
    high = value.astype(jnp.bfloat16)
    low = (value - high.astype(jnp.float32)).astype(jnp.bfloat16)
    return high, low


def dot(left, right):
    return jnp.dot(left, right, preferred_element_type=jnp.float32)


def dot3(left, right):
    return dot(left[0], right[0]) + (dot(left[0], right[1]) + dot(left[1], right[0]))


def dot_nt(left, right):
    return lax.dot_general(left, right, NT, preferred_element_type=jnp.float32)


def any_space(count):
    return [pl.BlockSpec(memory_space=pl.ANY)] * count


def vmem_space(count):
    return [pl.BlockSpec(memory_space=pltpu.VMEM)] * count


def cut_kernel(spec, *refs):
    owned, start, h_starts, width, masks, sources, w_mask = spec
    given, outs, sems = refs[:sources], refs[sources:-1], refs[-1]
    doc, feat = lax.axis_index("doc"), lax.axis_index("feat")
    copies = []
    for mask, out in zip(masks, outs):
        row = 0
        for ref, first in [(given[0], start)] + [(given[1], first) for first in h_starts]:
            rows = ref.shape[0]
            begin = pl.multiple_of((doc ^ mask) * owned + first, 128)
            copies.append((ref.at[:, pl.ds(begin, width)], out.at[pl.ds(row, rows), :]))
            row += rows
        if mask == w_mask:
            rows = out.shape[0] - row
            near = pl.multiple_of(feat * rows, 8)
            copies.append((given[2].at[pl.ds(near, rows), :], out.at[pl.ds(row, rows), :]))
    copies = [pltpu.make_async_copy(*pair, sems.at[i]) for i, pair in enumerate(copies)]
    for copy in copies:
        copy.start()
    for copy in copies:
        copy.wait()


def cut(given, owned, start, h_starts, width, masks, rows, w_mask, w_rows):
    spec = (owned, start, tuple(h_starts), width, tuple(masks), len(given), w_mask)
    count = (1 + len(h_starts)) * len(masks) + 1
    heights = [rows + w_rows * (mask == w_mask) for mask in masks]
    return pl.pallas_call(
        functools.partial(cut_kernel, spec),
        out_shape=[jax.ShapeDtypeStruct((height, width), jnp.float32) for height in heights],
        in_specs=any_space(len(given)),
        out_specs=vmem_space(len(masks)),
        scratch_shapes=[pltpu.SemaphoreType.DMA((count,))],
        cost_estimate=pl.CostEstimate(
            flops=0, bytes_accessed=8 * rows * width * len(masks), transcendentals=0
        ),
        name="cut_piece",
    )(*given)


def cut_plain(given, doc, feat, owned, start, h_starts, width, masks, rows, w_mask, w_rows):
    outs = []
    for mask in masks:
        begin = (doc ^ mask) * owned
        sources = [(given[0], start)] + [(given[1], first) for first in h_starts]
        parts = [lax.dynamic_slice(g, (0, begin + f), (g.shape[0], width)) for g, f in sources]
        if mask == w_mask:
            parts.append(lax.dynamic_slice_in_dim(given[2], feat * w_rows, w_rows, 0))
        outs.append(jnp.concatenate(parts, axis=0))
    return outs


def prepare_kernel(blocks, own_ref, *refs):
    part_refs, (high_ref, low_ref, high_t_ref, low_t_ref, sum_ref) = refs[:-5], refs[-5:]
    feat = lax.axis_index("feat")
    rows = own_ref.shape[0]
    part_rows = rows // len(part_refs)

    def place(value, row, count):
        near = pl.ds(row, count)
        high_ref[near, :], low_ref[near, :] = split(value)
        turned = value.T
        high_t_ref[:, near], low_t_ref[:, near] = split(turned)
        return jnp.sum(turned, axis=1, keepdims=True)

    total = place(own_ref[...], 0, rows)
    for mask, ref in enumerate(part_refs):
        at = (feat ^ mask) * part_rows
        for b in range(1, blocks):
            value = ref[(b - 1) * part_rows : b * part_rows, :]
            total = total + place(value, pl.multiple_of(b * rows + at, 128), part_rows)
    sum_ref[...] = total


def prepare(own, parts, blocks):
    rows, rank = own.shape
    docs = blocks * rows
    half = jnp.bfloat16
    shapes = [
        jax.ShapeDtypeStruct((docs, rank), half),
        jax.ShapeDtypeStruct((docs, rank), half),
        jax.ShapeDtypeStruct((rank, docs), half),
        jax.ShapeDtypeStruct((rank, docs), half),
        jax.ShapeDtypeStruct((rank, 1), jnp.float32),
    ]
    return pl.pallas_call(
        functools.partial(prepare_kernel, blocks),
        out_shape=shapes,
        in_specs=vmem_space(1 + len(parts)),
        out_specs=vmem_space(len(shapes)),
        compiler_params=pltpu.CompilerParams(vmem_limit_bytes=VMEM),
        cost_estimate=pl.CostEstimate(flops=0, bytes_accessed=docs * rank * 12, transcendentals=0),
        name="prepare_w",
    )(own, *parts)


def assemble(doc, h_blocks, h_ref):
    share = h_blocks[0].shape[0]
    for b, block in enumerate(h_blocks):
        h_ref[pl.ds(pl.multiple_of((doc ^ b) * share, 8), share), :] = block[...]
    return h_ref[...]


def ratio_of(m_ref, rows, weights, b, pair):
    near = slice(b * rows, (b + 1) * rows)
    return split(m_ref[:rows, :] / dot3((weights[0][near, :], weights[1][near, :]), pair))


def numerator(m_refs, rows, weights, which, pair, total):
    for m_ref, b in zip(m_refs, which):
        near = slice(b * rows, (b + 1) * rows)
        turned = (weights[2][:, near], weights[3][:, near])
        term = dot3(turned, ratio_of(m_ref, rows, weights, b, pair))
        total = term if total is None else total + term
    return total


def begin_kernel(blocks, rows, which, *refs):
    count = len(which)
    m_refs, h_blocks = refs[:count], refs[count : count + blocks]
    weights, total_ref, h_ref = refs[count + blocks : -2], refs[-2], refs[-1]
    factor = assemble(lax.axis_index("doc"), h_blocks, h_ref)
    total_ref[...] = numerator(m_refs, rows, weights, which, split(factor), None)


def piece_kernel(blocks, parts, rows, begun, first, *refs):
    m_refs, h_blocks = refs[:blocks], refs[blocks : 2 * blocks]
    weights, rest = refs[2 * blocks : 2 * blocks + 5], list(refs[2 * blocks + 5 :])
    begun_ref = rest.pop(0) if begun else None
    sums_in = (None, None) if first else (rest.pop(0), rest.pop(0))
    *back_refs, kept_out, sent_out, h_ref = rest
    width = h_ref.shape[1]
    share = h_blocks[0].shape[0]
    part_rows = rows // parts
    doc, feat = lax.axis_index("doc"), lax.axis_index("feat")
    even = (feat & 1) == 0

    factor = assemble(doc, h_blocks, h_ref)
    for step in range(INNER):
        pair = split(factor)
        which = [b for b in range(blocks) if step or b not in begun]
        total = begun_ref[...] if begun and not step else None
        total = numerator([m_refs[b] for b in which], rows, weights, which, pair, total)
        factor = factor * total / weights[4][...]
    h_ref[...] = factor
    for b in range(blocks):
        back_refs[b][...] = h_ref[pl.ds(pl.multiple_of((doc ^ b) * share, 8), share), :]
    pair = split(factor)
    ones = jnp.ones((PAD, width), jnp.bfloat16)
    row_sum = dot_nt(ones, pair[0]) + dot_nt(ones, pair[1])

    def put(b, half, near, left, right):
        kept, gone = jnp.where(even, left, right), jnp.where(even, right, left)
        for value, out, before in ((kept, kept_out, sums_in[0]), (gone, sent_out, sums_in[1])):
            out[b, half, near, :] = value if first else before[b, half, near, :] + value

    for b in range(blocks):
        high, low = ratio_of(m_refs[b], rows, weights, b, pair)
        term = dot_nt(high, pair[0]) + (dot_nt(high, pair[1]) + dot_nt(low, pair[0]))
        for half in range(parts // 2):
            at = 2 * half * part_rows
            left, right = term[at : at + part_rows, :], term[at + part_rows : at + 2 * part_rows, :]
            put(b, half, slice(0, part_rows), left, right)
            put(b, half, slice(part_rows, part_rows + PAD), row_sum, row_sum)


def update_piece(m_blocks, h_blocks, rows, weights, sums, parts, early):
    blocks = len(m_blocks)
    width = m_blocks[0].shape[1]
    rank = weights[0].shape[1]
    share = rank // blocks
    first = sums is None
    half_shape = jax.ShapeDtypeStruct((blocks, parts // 2, rows // parts + PAD, rank), jnp.float32)
    back_shape = jax.ShapeDtypeStruct((share, width), jnp.float32)
    total_shape = jax.ShapeDtypeStruct((rank, width), jnp.float32)
    extra = {
        "scratch_shapes": [pltpu.VMEM((rank, width), jnp.float32)],
        "compiler_params": pltpu.CompilerParams(vmem_limit_bytes=VMEM),
    }

    def cost(dots):
        return pl.CostEstimate(
            flops=2 * dots * blocks * rows * width * rank,
            bytes_accessed=blocks * rows * (4 * width + 16 * rank),
            transcendentals=0,
        )

    begun = []
    if early:
        begun = [
            pl.pallas_call(
                functools.partial(begin_kernel, blocks, rows, early),
                out_shape=total_shape,
                in_specs=vmem_space(len(early) + blocks + 5),
                out_specs=vmem_space(1)[0],
                cost_estimate=cost(6),
                name="begin_piece",
                **extra,
            )(*[m_blocks[b] for b in early], *h_blocks, *weights)
        ]
    sums = [] if first else list(sums)
    given = [*m_blocks, *h_blocks, *weights, *begun, *sums]
    *backs, kept, sent = pl.pallas_call(
        functools.partial(piece_kernel, blocks, parts, rows, early, first),
        out_shape=[back_shape] * blocks + [half_shape] * 2,
        in_specs=vmem_space(len(given)),
        out_specs=vmem_space(blocks + 2),
        input_output_aliases={} if first else {len(given) - 2 + i: blocks + i for i in range(2)},
        cost_estimate=cost(15),
        name="update_piece",
        **extra,
    )(*given)
    return backs, (kept, sent)


def update_plain(m_blocks, h_blocks, rows, whole_w, sums, parts, doc, feat):
    highest = lax.Precision.HIGHEST
    blocks, rank = len(m_blocks), whole_w.shape[1]
    share, width = rank // blocks, m_blocks[0].shape[1]
    whole_m = jnp.concatenate([m[:rows] for m in m_blocks], axis=0)
    factor = jnp.zeros((rank, width), jnp.float32)
    for k in range(blocks):
        factor = lax.dynamic_update_slice(factor, h_blocks[k], ((doc ^ k) * share, 0))
    column = jnp.sum(whole_w, axis=0)[:, None]
    for _ in range(INNER):
        ratio = whole_m / jnp.dot(whole_w, factor, precision=highest)
        numer = lax.dot_general(whole_w, ratio, (((0,), (0,)), ((), ())), precision=highest)
        factor = factor * numer / column
    ratio = whole_m / jnp.dot(whole_w, factor, precision=highest)
    wnumer = lax.dot_general(ratio, factor, NT, precision=highest)
    wnumer = wnumer.reshape(blocks, parts, rows // parts, rank)
    row_sum = jnp.broadcast_to(jnp.sum(factor, axis=1), (blocks, parts, PAD, rank))
    more = jnp.concatenate([wnumer, row_sum], axis=2)
    more = more.reshape(blocks, parts // 2, 2, *more.shape[2:])
    halves = [lax.dynamic_index_in_dim(more, (feat & 1) ^ i, 2, keepdims=False) for i in range(2)]
    if sums is not None:
        halves = [old + new for old, new in zip(sums, halves)]
    backs = [lax.dynamic_slice_in_dim(factor, (doc ^ k) * share, share, 0) for k in range(blocks)]
    return backs, halves


def spread_feat(value, bits):
    got = {0: value}
    for j in reversed(range(bits)):
        for mask, held in list(got.items()):
            pairs = xor_pairs(1 << bits, 1 << j)
            got[mask | 1 << j] = lax.ppermute(held, "feat", pairs)
    return [got[mask] for mask in range(1 << bits)]


def in_order(parts, feat):
    rows = parts[0].shape[0]
    whole = jnp.zeros((rows * len(parts), *parts[0].shape[1:]), parts[0].dtype)
    for mask, part in enumerate(parts):
        whole = lax.dynamic_update_slice_in_dim(whole, part, (feat ^ mask) * rows, 0)
    return whole


def add_feat(kept, sent, bits, feat):
    held = [kept, lax.ppermute(sent, "feat", xor_pairs(1 << bits, 1))]
    shape = kept.shape
    held = [h.reshape((shape[0],) + (2,) * (bits - 1) + shape[2:]) for h in held]
    for j in range(1, bits):
        bit = (feat >> j) & 1
        axis = bits - j

        def half(side):
            return sum(lax.dynamic_index_in_dim(h, side, axis, keepdims=False) for h in held)

        other = lax.ppermute(half(1 - bit), "feat", xor_pairs(1 << bits, 1 << j))
        held = [half(bit), other]
    return held


def after(value, earlier):
    return lax.optimization_barrier((value, *earlier))[0] if earlier else value


def piece_widths(owned):
    return [owned] if owned % WIDTH else [WIDTH] * (owned // WIDTH)


def body(n_doc, n_feat, matrix, doc_factor, feat_factor):
    doc, feat = lax.axis_index("doc"), lax.axis_index("feat")
    bits = n_feat.bit_length() - 1
    rows, columns = matrix.shape
    share, rank = feat_factor.shape[0], doc_factor.shape[1]
    owned = columns // n_doc
    widths = piece_widths(owned)
    pieces = len(widths)
    starts = [sum(widths[:p]) for p in range(pieces)]
    part_rows = rows // n_feat
    others = list(range(n_doc - 1, 0, -1))
    in_kernel = n_doc * rows * rank * 32 < VMEM and widths[0] % 128 == 0 and part_rows % 128 == 0
    w_rides = widths[0] == rank

    def send(value, k):
        return lax.ppermute(value, "doc", xor_pairs(n_doc, k)) if k else value

    riders = [[0, 1][:pieces]] + [[p + 1] if p + 1 < pieces else [] for p in range(1, pieces)]
    w_row = rows + share * len(riders[0])

    def m_piece(p, *earlier):
        given = [after(matrix, earlier), feat_factor]
        height = rows + share * len(riders[p])
        w_mask = n_doc // 2 if w_rides and p == 0 else -1
        given += [doc_factor] if w_mask > 0 else []
        masks = [*others, 0]
        place = (owned, starts[p], [starts[q] for q in riders[p]], widths[p], masks, height)
        place += (w_mask, part_rows)
        arrays = cut(given, *place) if in_kernel else cut_plain(given, doc, feat, *place)
        got = {k: send(piece, k) for k, piece in zip(masks, arrays)}
        return [got[k] for k in range(n_doc)]

    m_pieces = []
    for p in range(pieces):
        gate = m_pieces[p - 2][1:] if p > 1 else m_pieces[0][1:2] if p else []
        m_pieces.append(m_piece(p, *gate))

    w_part = lax.dynamic_slice_in_dim(doc_factor, feat * part_rows, part_rows, 0)
    far = n_doc // 2
    got = {0: w_part, far: m_pieces[0][far][w_row:] if w_rides else send(w_part, far)}
    while far > 1:
        far //= 2
        got |= {mask | far: send(held, far) for mask, held in got.items()}
    w_parts = [got[k] for k in range(1, n_doc)]
    w_parts = spread_feat(jnp.concatenate(w_parts, axis=0), bits)
    if in_kernel:
        weights = prepare(doc_factor, w_parts, n_doc)
    else:
        w_parts = [w.reshape(n_doc - 1, part_rows, rank).swapaxes(0, 1) for w in w_parts]
        w_others = in_order(w_parts, feat).swapaxes(0, 1).reshape(-1, rank)
        whole_w = jnp.concatenate([doc_factor, w_others], axis=0)

    sums = None
    backs = []
    for p in range(pieces):
        source = 0 if p < 2 else p - 1
        at = rows + share * (p == 1)
        ready = backs[-1][:1] if backs else []
        h_blocks = [after(m[at : at + share], ready) for m in m_pieces[source]]
        place = (m_pieces[p], h_blocks, rows)
        if in_kernel:
            early = list(range(n_doc - 1)) if p and p == pieces - 1 else []
            rows_back, sums = update_piece(*place, weights, sums, n_feat, early)
        else:
            rows_back, sums = update_plain(*place, whole_w, sums, n_feat, doc, feat)
        backs.append(rows_back)

    kept, other = add_feat(*sums, bits, feat)
    batches = [b for b in (backs[:-1], backs[-1:]) if b]

    def give_back(batch, *earlier):
        rows_of = [jnp.concatenate([b[k] for b in batch], axis=0) for k in range(n_doc)]
        return [send(after(r, earlier), k) for k, r in enumerate(rows_of)]

    returned = [give_back(b) for b in batches[:-1]]
    kept = after(kept, [r for rows_of in returned for r in rows_of[1:]])
    total = kept[0] + other[0]
    for k in range(1, n_doc):
        total = total + send(kept[k] + other[k], k)
    returned.append(give_back(batches[-1], total))
    new_part = w_part * total[:part_rows] / total[part_rows]
    new_parts = spread_feat(new_part, bits)
    new_doc = in_order(new_parts, feat)
    new_feat = jnp.zeros((share, columns), jnp.float32)
    start = 0
    for batch, rows_of in zip(batches, returned):
        for k, value in enumerate(rows_of):
            value = value.reshape(len(batch), share, -1).swapaxes(0, 1).reshape(share, -1)
            value = after(value, new_parts[-1:])
            new_feat = lax.dynamic_update_slice(new_feat, value, (0, (doc ^ k) * owned + start))
        start += value.shape[1]
    return new_doc, new_feat


def solution(mesh):
    placed = (P(("grp", "doc"), "feat"), P(("grp", "doc"), None), P(("grp", "doc"), "feat"))
    return jax.shard_map(
        functools.partial(body, mesh.shape["doc"], mesh.shape["feat"]),
        mesh=mesh,
        in_specs=placed,
        out_specs=(P(("grp", "doc"), None), P(("grp", "doc"), "feat")),
        check_vma=False,
    )
```

```python
import functools

import jax
import jax.numpy as jnp
from jax import lax
from jax.experimental import pallas as pl
from jax.experimental.pallas import tpu as pltpu
from jax.sharding import PartitionSpec as P

INNER = 2
WIDTH = 256
PAD = 8
VMEM = 20 * 1024 * 1024
NT = (((1,), (1,)), ((), ()))


def xor_pairs(count, mask):
    return [(i, i ^ mask) for i in range(count)]


def split(value):
    high = value.astype(jnp.bfloat16)
    low = (value - high.astype(jnp.float32)).astype(jnp.bfloat16)
    return high, low


def dot(left, right):
    return jnp.dot(left, right, preferred_element_type=jnp.float32)


def dot3(left, right):
    return dot(left[0], right[0]) + (dot(left[0], right[1]) + dot(left[1], right[0]))


def dot_nt(left, right):
    return lax.dot_general(left, right, NT, preferred_element_type=jnp.float32)


def any_space(count):
    return [pl.BlockSpec(memory_space=pl.ANY)] * count


def vmem_space(count):
    return [pl.BlockSpec(memory_space=pltpu.VMEM)] * count


def cut_kernel(spec, *refs):
    owned, start, h_starts, width, masks, sources, w_mask = spec
    given, outs, sems = refs[:sources], refs[sources:-1], refs[-1]
    doc, feat = lax.axis_index("doc"), lax.axis_index("feat")
    copies = []
    for mask, out in zip(masks, outs):
        row = 0
        for ref, first in [(given[0], start)] + [(given[1], first) for first in h_starts]:
            rows = ref.shape[0]
            begin = pl.multiple_of((doc ^ mask) * owned + first, 128)
            copies.append((ref.at[:, pl.ds(begin, width)], out.at[pl.ds(row, rows), :]))
            row += rows
        if mask == w_mask:
            rows = out.shape[0] - row
            near = pl.multiple_of(feat * rows, 8)
            copies.append((given[2].at[pl.ds(near, rows), :], out.at[pl.ds(row, rows), :]))
    copies = [pltpu.make_async_copy(*pair, sems.at[i]) for i, pair in enumerate(copies)]
    for copy in copies:
        copy.start()
    for copy in copies:
        copy.wait()


def cut(given, owned, start, h_starts, width, masks, rows, w_mask, w_rows):
    spec = (owned, start, tuple(h_starts), width, tuple(masks), len(given), w_mask)
    count = (1 + len(h_starts)) * len(masks) + 1
    heights = [rows + w_rows * (mask == w_mask) for mask in masks]
    return pl.pallas_call(
        functools.partial(cut_kernel, spec),
        out_shape=[jax.ShapeDtypeStruct((height, width), jnp.float32) for height in heights],
        in_specs=any_space(len(given)),
        out_specs=vmem_space(len(masks)),
        scratch_shapes=[pltpu.SemaphoreType.DMA((count,))],
        cost_estimate=pl.CostEstimate(
            flops=0, bytes_accessed=8 * rows * width * len(masks), transcendentals=0
        ),
        name="cut_piece",
    )(*given)


def cut_plain(given, doc, feat, owned, start, h_starts, width, masks, rows, w_mask, w_rows):
    outs = []
    for mask in masks:
        begin = (doc ^ mask) * owned
        sources = [(given[0], start)] + [(given[1], first) for first in h_starts]
        parts = [lax.dynamic_slice(g, (0, begin + f), (g.shape[0], width)) for g, f in sources]
        if mask == w_mask:
            parts.append(lax.dynamic_slice_in_dim(given[2], feat * w_rows, w_rows, 0))
        outs.append(jnp.concatenate(parts, axis=0))
    return outs


def prepare_kernel(blocks, own_ref, *refs):
    part_refs, (high_ref, low_ref, high_t_ref, low_t_ref, sum_ref) = refs[:-5], refs[-5:]
    feat = lax.axis_index("feat")
    rows = own_ref.shape[0]
    part_rows = rows // len(part_refs)

    def place(value, row, count):
        near = pl.ds(row, count)
        high_ref[near, :], low_ref[near, :] = split(value)
        turned = value.T
        high_t_ref[:, near], low_t_ref[:, near] = split(turned)
        return jnp.sum(turned, axis=1, keepdims=True)

    total = place(own_ref[...], 0, rows)
    for mask, ref in enumerate(part_refs):
        at = (feat ^ mask) * part_rows
        for b in range(1, blocks):
            value = ref[(b - 1) * part_rows : b * part_rows, :]
            total = total + place(value, pl.multiple_of(b * rows + at, 128), part_rows)
    sum_ref[...] = total


def prepare(own, parts, blocks):
    rows, rank = own.shape
    docs = blocks * rows
    half = jnp.bfloat16
    shapes = [
        jax.ShapeDtypeStruct((docs, rank), half),
        jax.ShapeDtypeStruct((docs, rank), half),
        jax.ShapeDtypeStruct((rank, docs), half),
        jax.ShapeDtypeStruct((rank, docs), half),
        jax.ShapeDtypeStruct((rank, 1), jnp.float32),
    ]
    return pl.pallas_call(
        functools.partial(prepare_kernel, blocks),
        out_shape=shapes,
        in_specs=vmem_space(1 + len(parts)),
        out_specs=vmem_space(len(shapes)),
        compiler_params=pltpu.CompilerParams(vmem_limit_bytes=VMEM),
        cost_estimate=pl.CostEstimate(flops=0, bytes_accessed=docs * rank * 12, transcendentals=0),
        name="prepare_w",
    )(own, *parts)


def assemble(doc, h_blocks, h_ref):
    share = h_blocks[0].shape[0]
    for b, block in enumerate(h_blocks):
        h_ref[pl.ds(pl.multiple_of((doc ^ b) * share, 8), share), :] = block[...]
    return h_ref[...]


def ratio_of(m_ref, rows, weights, b, pair):
    near = slice(b * rows, (b + 1) * rows)
    return split(m_ref[:rows, :] / dot3((weights[0][near, :], weights[1][near, :]), pair))


def numerator(m_refs, rows, weights, which, pair, total):
    for m_ref, b in zip(m_refs, which):
        near = slice(b * rows, (b + 1) * rows)
        turned = (weights[2][:, near], weights[3][:, near])
        term = dot3(turned, ratio_of(m_ref, rows, weights, b, pair))
        total = term if total is None else total + term
    return total


def begin_kernel(blocks, rows, which, *refs):
    count = len(which)
    m_refs, h_blocks = refs[:count], refs[count : count + blocks]
    weights, total_ref, h_ref = refs[count + blocks : -2], refs[-2], refs[-1]
    factor = assemble(lax.axis_index("doc"), h_blocks, h_ref)
    total_ref[...] = numerator(m_refs, rows, weights, which, split(factor), None)


def piece_kernel(blocks, parts, rows, begun, first, *refs):
    m_refs, h_blocks = refs[:blocks], refs[blocks : 2 * blocks]
    weights, rest = refs[2 * blocks : 2 * blocks + 5], list(refs[2 * blocks + 5 :])
    begun_ref = rest.pop(0) if begun else None
    sums_in = (None, None) if first else (rest.pop(0), rest.pop(0))
    *back_refs, kept_out, sent_out, h_ref = rest
    width = h_ref.shape[1]
    share = h_blocks[0].shape[0]
    part_rows = rows // parts
    doc, feat = lax.axis_index("doc"), lax.axis_index("feat")
    even = (feat & 1) == 0

    factor = assemble(doc, h_blocks, h_ref)
    for step in range(INNER):
        pair = split(factor)
        which = [b for b in range(blocks) if step or b not in begun]
        total = begun_ref[...] if begun and not step else None
        total = numerator([m_refs[b] for b in which], rows, weights, which, pair, total)
        factor = factor * total / weights[4][...]
    h_ref[...] = factor
    for b in range(blocks):
        back_refs[b][...] = h_ref[pl.ds(pl.multiple_of((doc ^ b) * share, 8), share), :]
    pair = split(factor)
    ones = jnp.ones((PAD, width), jnp.bfloat16)
    row_sum = dot_nt(ones, pair[0]) + dot_nt(ones, pair[1])

    def put(b, half, near, left, right):
        kept, gone = jnp.where(even, left, right), jnp.where(even, right, left)
        for value, out, before in ((kept, kept_out, sums_in[0]), (gone, sent_out, sums_in[1])):
            out[b, half, near, :] = value if first else before[b, half, near, :] + value

    for b in range(blocks):
        high, low = ratio_of(m_refs[b], rows, weights, b, pair)
        term = dot_nt(high, pair[0]) + (dot_nt(high, pair[1]) + dot_nt(low, pair[0]))
        for half in range(parts // 2):
            at = 2 * half * part_rows
            left, right = term[at : at + part_rows, :], term[at + part_rows : at + 2 * part_rows, :]
            put(b, half, slice(0, part_rows), left, right)
            put(b, half, slice(part_rows, part_rows + PAD), row_sum, row_sum)


def update_piece(m_blocks, h_blocks, rows, weights, sums, parts, early):
    blocks = len(m_blocks)
    width = m_blocks[0].shape[1]
    rank = weights[0].shape[1]
    share = rank // blocks
    first = sums is None
    half_shape = jax.ShapeDtypeStruct((blocks, parts // 2, rows // parts + PAD, rank), jnp.float32)
    back_shape = jax.ShapeDtypeStruct((share, width), jnp.float32)
    total_shape = jax.ShapeDtypeStruct((rank, width), jnp.float32)
    extra = {
        "scratch_shapes": [pltpu.VMEM((rank, width), jnp.float32)],
        "compiler_params": pltpu.CompilerParams(vmem_limit_bytes=VMEM),
    }

    def cost(dots):
        return pl.CostEstimate(
            flops=2 * dots * blocks * rows * width * rank,
            bytes_accessed=blocks * rows * (4 * width + 16 * rank),
            transcendentals=0,
        )

    begun = []
    if early:
        begun = [
            pl.pallas_call(
                functools.partial(begin_kernel, blocks, rows, early),
                out_shape=total_shape,
                in_specs=vmem_space(len(early) + blocks + 5),
                out_specs=vmem_space(1)[0],
                cost_estimate=cost(6),
                name="begin_piece",
                **extra,
            )(*[m_blocks[b] for b in early], *h_blocks, *weights)
        ]
    sums = [] if first else list(sums)
    given = [*m_blocks, *h_blocks, *weights, *begun, *sums]
    *backs, kept, sent = pl.pallas_call(
        functools.partial(piece_kernel, blocks, parts, rows, early, first),
        out_shape=[back_shape] * blocks + [half_shape] * 2,
        in_specs=vmem_space(len(given)),
        out_specs=vmem_space(blocks + 2),
        input_output_aliases={} if first else {len(given) - 2 + i: blocks + i for i in range(2)},
        cost_estimate=cost(15),
        name="update_piece",
        **extra,
    )(*given)
    return backs, (kept, sent), begun


def update_plain(m_blocks, h_blocks, rows, whole_w, sums, parts, doc, feat):
    highest = lax.Precision.HIGHEST
    blocks, rank = len(m_blocks), whole_w.shape[1]
    share, width = rank // blocks, m_blocks[0].shape[1]
    whole_m = jnp.concatenate([m[:rows] for m in m_blocks], axis=0)
    factor = jnp.zeros((rank, width), jnp.float32)
    for k in range(blocks):
        factor = lax.dynamic_update_slice(factor, h_blocks[k], ((doc ^ k) * share, 0))
    column = jnp.sum(whole_w, axis=0)[:, None]
    for _ in range(INNER):
        ratio = whole_m / jnp.dot(whole_w, factor, precision=highest)
        numer = lax.dot_general(whole_w, ratio, (((0,), (0,)), ((), ())), precision=highest)
        factor = factor * numer / column
    ratio = whole_m / jnp.dot(whole_w, factor, precision=highest)
    wnumer = lax.dot_general(ratio, factor, NT, precision=highest)
    wnumer = wnumer.reshape(blocks, parts, rows // parts, rank)
    row_sum = jnp.broadcast_to(jnp.sum(factor, axis=1), (blocks, parts, PAD, rank))
    more = jnp.concatenate([wnumer, row_sum], axis=2)
    more = more.reshape(blocks, parts // 2, 2, *more.shape[2:])
    halves = [lax.dynamic_index_in_dim(more, (feat & 1) ^ i, 2, keepdims=False) for i in range(2)]
    if sums is not None:
        halves = [old + new for old, new in zip(sums, halves)]
    backs = [lax.dynamic_slice_in_dim(factor, (doc ^ k) * share, share, 0) for k in range(blocks)]
    return backs, halves, []


def spread_feat(value, bits):
    got = {0: value}
    for j in reversed(range(bits)):
        for mask, held in list(got.items()):
            pairs = xor_pairs(1 << bits, 1 << j)
            got[mask | 1 << j] = lax.ppermute(held, "feat", pairs)
    return [got[mask] for mask in range(1 << bits)]


def in_order(parts, feat):
    rows = parts[0].shape[0]
    whole = jnp.zeros((rows * len(parts), *parts[0].shape[1:]), parts[0].dtype)
    for mask, part in enumerate(parts):
        whole = lax.dynamic_update_slice_in_dim(whole, part, (feat ^ mask) * rows, 0)
    return whole


def add_feat(kept, sent, bits, feat):
    held = [kept, lax.ppermute(sent, "feat", xor_pairs(1 << bits, 1))]
    shape = kept.shape
    held = [h.reshape((shape[0],) + (2,) * (bits - 1) + shape[2:]) for h in held]
    for j in range(1, bits):
        bit = (feat >> j) & 1
        axis = bits - j

        def half(side):
            return sum(lax.dynamic_index_in_dim(h, side, axis, keepdims=False) for h in held)

        other = lax.ppermute(half(1 - bit), "feat", xor_pairs(1 << bits, 1 << j))
        held = [half(bit), other]
    return held


def after(value, earlier):
    return lax.optimization_barrier((value, *earlier))[0] if earlier else value


def piece_widths(owned):
    return [owned] if owned % WIDTH else [WIDTH] * (owned // WIDTH)


def body(n_doc, n_feat, matrix, doc_factor, feat_factor):
    doc, feat = lax.axis_index("doc"), lax.axis_index("feat")
    bits = n_feat.bit_length() - 1
    rows, columns = matrix.shape
    share, rank = feat_factor.shape[0], doc_factor.shape[1]
    owned = columns // n_doc
    widths = piece_widths(owned)
    pieces = len(widths)
    starts = [sum(widths[:p]) for p in range(pieces)]
    part_rows = rows // n_feat
    others = list(range(n_doc - 1, 0, -1))
    in_kernel = n_doc * rows * rank * 32 < VMEM and widths[0] % 128 == 0 and part_rows % 128 == 0
    w_rides = widths[0] == rank

    def send(value, k):
        return lax.ppermute(value, "doc", xor_pairs(n_doc, k)) if k else value

    riders = [[0, 1][:pieces]] + [[p + 1] if p + 1 < pieces else [] for p in range(1, pieces)]
    w_row = rows + share * len(riders[0])

    def m_piece(p, *earlier):
        given = [after(matrix, earlier), feat_factor]
        height = rows + share * len(riders[p])
        w_mask = n_doc // 2 if w_rides and p == 0 else -1
        given += [doc_factor] if w_mask > 0 else []
        masks = [*others, 0]
        place = (owned, starts[p], [starts[q] for q in riders[p]], widths[p], masks, height)
        place += (w_mask, part_rows)
        arrays = cut(given, *place) if in_kernel else cut_plain(given, doc, feat, *place)
        got = {k: send(piece, k) for k, piece in zip(masks, arrays)}
        return [got[k] for k in range(n_doc)]

    m_pieces = []
    for p in range(pieces):
        gate = m_pieces[p - 2][1:] if p > 1 else m_pieces[0][1:2] if p else []
        m_pieces.append(m_piece(p, *gate))

    w_part = lax.dynamic_slice_in_dim(doc_factor, feat * part_rows, part_rows, 0)
    far = n_doc // 2
    got = {0: w_part, far: m_pieces[0][far][w_row:] if w_rides else send(w_part, far)}
    while far > 1:
        far //= 2
        got |= {mask | far: send(held, far) for mask, held in got.items()}
    w_parts = [got[k] for k in range(1, n_doc)]
    w_parts = spread_feat(jnp.concatenate(w_parts, axis=0), bits)
    if in_kernel:
        weights = prepare(doc_factor, w_parts, n_doc)
    else:
        w_parts = [w.reshape(n_doc - 1, part_rows, rank).swapaxes(0, 1) for w in w_parts]
        w_others = in_order(w_parts, feat).swapaxes(0, 1).reshape(-1, rank)
        whole_w = jnp.concatenate([doc_factor, w_others], axis=0)

    sums = None
    backs = []
    for p in range(pieces):
        source = 0 if p < 2 else p - 1
        at = rows + share * (p == 1)
        ready = backs[-1][:1] if backs else []
        h_blocks = [after(m[at : at + share], ready) for m in m_pieces[source]]
        place = (m_pieces[p], h_blocks, rows)
        if in_kernel:
            early = list(range(n_doc - 1)) if p and p == pieces - 1 else []
            rows_back, sums, begun = update_piece(*place, weights, sums, n_feat, early)
        else:
            rows_back, sums, begun = update_plain(*place, whole_w, sums, n_feat, doc, feat)
        backs.append(rows_back)

    def give_back(batch, *earlier):
        rows_of = [jnp.concatenate([b[k] for b in batch], axis=0) for k in range(n_doc)]
        return [send(after(r, earlier), k) for k, r in enumerate(rows_of)]

    batches = [b for b in (backs[:1], backs[1:]) if b]
    returned = [give_back(b, *begun) for b in batches[:-1]]
    kept, sent = sums
    kept, other = add_feat(kept, after(sent, [r for got in returned for r in got[1:]]), bits, feat)
    returned.append(give_back(batches[-1]))
    kept = after(kept, returned[-1][1:])
    total = kept[0] + other[0]
    for k in range(1, n_doc):
        total = total + send(kept[k] + other[k], k)
    new_part = w_part * total[:part_rows] / total[part_rows]
    new_parts = spread_feat(new_part, bits)
    new_doc = in_order(new_parts, feat)
    new_feat = jnp.zeros((share, columns), jnp.float32)
    start = 0
    for batch, rows_of in zip(batches, returned):
        for k, value in enumerate(rows_of):
            value = value.reshape(len(batch), share, -1).swapaxes(0, 1).reshape(share, -1)
            value = after(value, new_parts[-1:])
            new_feat = lax.dynamic_update_slice(new_feat, value, (0, (doc ^ k) * owned + start))
        start += value.shape[1]
    return new_doc, new_feat


def solution(mesh):
    placed = (P(("grp", "doc"), "feat"), P(("grp", "doc"), None), P(("grp", "doc"), "feat"))
    return jax.shard_map(
        functools.partial(body, mesh.shape["doc"], mesh.shape["feat"]),
        mesh=mesh,
        in_specs=placed,
        out_specs=(P(("grp", "doc"), None), P(("grp", "doc"), "feat")),
        check_vma=False,
    )
```

```python
import functools

import jax
import jax.numpy as jnp
from jax import lax
from jax.experimental import pallas as pl
from jax.experimental.pallas import tpu as pltpu
from jax.sharding import PartitionSpec as P

INNER = 2
WIDTH = 256
PAD = 8
VMEM = 20 * 1024 * 1024
NT = (((1,), (1,)), ((), ()))


def xor_pairs(count, mask):
    return [(i, i ^ mask) for i in range(count)]


def split(value):
    high = value.astype(jnp.bfloat16)
    low = (value - high.astype(jnp.float32)).astype(jnp.bfloat16)
    return high, low


def dot(left, right):
    return jnp.dot(left, right, preferred_element_type=jnp.float32)


def dot3(left, right):
    return dot(left[0], right[0]) + (dot(left[0], right[1]) + dot(left[1], right[0]))


def dot_nt(left, right):
    return lax.dot_general(left, right, NT, preferred_element_type=jnp.float32)


def any_space(count):
    return [pl.BlockSpec(memory_space=pl.ANY)] * count


def vmem_space(count):
    return [pl.BlockSpec(memory_space=pltpu.VMEM)] * count


def cut_kernel(spec, *refs):
    owned, start, h_starts, width, masks, sources, w_mask = spec
    given, outs, sems = refs[:sources], refs[sources:-1], refs[-1]
    doc, feat = lax.axis_index("doc"), lax.axis_index("feat")
    copies = []
    for mask, out in zip(masks, outs):
        row = 0
        for ref, first in [(given[0], start)] + [(given[1], first) for first in h_starts]:
            rows = ref.shape[0]
            begin = pl.multiple_of((doc ^ mask) * owned + first, 128)
            copies.append((ref.at[:, pl.ds(begin, width)], out.at[pl.ds(row, rows), :]))
            row += rows
        if mask == w_mask:
            rows = out.shape[0] - row
            near = pl.multiple_of(feat * rows, 8)
            copies.append((given[2].at[pl.ds(near, rows), :], out.at[pl.ds(row, rows), :]))
    copies = [pltpu.make_async_copy(*pair, sems.at[i]) for i, pair in enumerate(copies)]
    for copy in copies:
        copy.start()
    for copy in copies:
        copy.wait()


def cut(given, owned, start, h_starts, width, masks, rows, w_mask, w_rows):
    spec = (owned, start, tuple(h_starts), width, tuple(masks), len(given), w_mask)
    count = (1 + len(h_starts)) * len(masks) + 1
    heights = [rows + w_rows * (mask == w_mask) for mask in masks]
    return pl.pallas_call(
        functools.partial(cut_kernel, spec),
        out_shape=[jax.ShapeDtypeStruct((height, width), jnp.float32) for height in heights],
        in_specs=any_space(len(given)),
        out_specs=vmem_space(len(masks)),
        scratch_shapes=[pltpu.SemaphoreType.DMA((count,))],
        cost_estimate=pl.CostEstimate(
            flops=0, bytes_accessed=8 * rows * width * len(masks), transcendentals=0
        ),
        name="cut_piece",
    )(*given)


def cut_plain(given, doc, feat, owned, start, h_starts, width, masks, rows, w_mask, w_rows):
    outs = []
    for mask in masks:
        begin = (doc ^ mask) * owned
        sources = [(given[0], start)] + [(given[1], first) for first in h_starts]
        parts = [lax.dynamic_slice(g, (0, begin + f), (g.shape[0], width)) for g, f in sources]
        if mask == w_mask:
            parts.append(lax.dynamic_slice_in_dim(given[2], feat * w_rows, w_rows, 0))
        outs.append(jnp.concatenate(parts, axis=0))
    return outs


def prepare_kernel(blocks, own_ref, *refs):
    part_refs, (high_ref, low_ref, high_t_ref, low_t_ref, sum_ref) = refs[:-5], refs[-5:]
    feat = lax.axis_index("feat")
    rows = own_ref.shape[0]
    part_rows = rows // len(part_refs)

    def place(value, row, count):
        near = pl.ds(row, count)
        high_ref[near, :], low_ref[near, :] = split(value)
        turned = value.T
        high_t_ref[:, near], low_t_ref[:, near] = split(turned)
        return jnp.sum(turned, axis=1, keepdims=True)

    total = place(own_ref[...], 0, rows)
    for mask, ref in enumerate(part_refs):
        at = (feat ^ mask) * part_rows
        for b in range(1, blocks):
            value = ref[(b - 1) * part_rows : b * part_rows, :]
            total = total + place(value, pl.multiple_of(b * rows + at, 128), part_rows)
    sum_ref[...] = total


def prepare(own, parts, blocks):
    rows, rank = own.shape
    docs = blocks * rows
    half = jnp.bfloat16
    shapes = [
        jax.ShapeDtypeStruct((docs, rank), half),
        jax.ShapeDtypeStruct((docs, rank), half),
        jax.ShapeDtypeStruct((rank, docs), half),
        jax.ShapeDtypeStruct((rank, docs), half),
        jax.ShapeDtypeStruct((rank, 1), jnp.float32),
    ]
    return pl.pallas_call(
        functools.partial(prepare_kernel, blocks),
        out_shape=shapes,
        in_specs=vmem_space(1 + len(parts)),
        out_specs=vmem_space(len(shapes)),
        compiler_params=pltpu.CompilerParams(vmem_limit_bytes=VMEM),
        cost_estimate=pl.CostEstimate(flops=0, bytes_accessed=docs * rank * 12, transcendentals=0),
        name="prepare_w",
    )(own, *parts)


def assemble(doc, h_blocks, h_ref):
    share = h_blocks[0].shape[0]
    for b, block in enumerate(h_blocks):
        h_ref[pl.ds(pl.multiple_of((doc ^ b) * share, 8), share), :] = block[...]
    return h_ref[...]


def ratio_of(m_ref, rows, weights, b, pair):
    near = slice(b * rows, (b + 1) * rows)
    return split(m_ref[:rows, :] / dot3((weights[0][near, :], weights[1][near, :]), pair))


def numerator(m_refs, rows, weights, which, pair, total):
    for m_ref, b in zip(m_refs, which):
        near = slice(b * rows, (b + 1) * rows)
        turned = (weights[2][:, near], weights[3][:, near])
        term = dot3(turned, ratio_of(m_ref, rows, weights, b, pair))
        total = term if total is None else total + term
    return total


def begin_kernel(blocks, rows, which, *refs):
    count = len(which)
    m_refs, h_blocks = refs[:count], refs[count : count + blocks]
    weights, total_ref, h_ref = refs[count + blocks : -2], refs[-2], refs[-1]
    factor = assemble(lax.axis_index("doc"), h_blocks, h_ref)
    total_ref[...] = numerator(m_refs, rows, weights, which, split(factor), None)


def piece_kernel(blocks, parts, rows, begun, first, *refs):
    m_refs, h_blocks = refs[:blocks], refs[blocks : 2 * blocks]
    weights, rest = refs[2 * blocks : 2 * blocks + 5], list(refs[2 * blocks + 5 :])
    begun_ref = rest.pop(0) if begun else None
    sums_in = (None, None) if first else (rest.pop(0), rest.pop(0))
    *back_refs, kept_out, sent_out, h_ref = rest
    width = h_ref.shape[1]
    share = h_blocks[0].shape[0]
    part_rows = rows // parts
    doc, feat = lax.axis_index("doc"), lax.axis_index("feat")
    even = (feat & 1) == 0

    factor = assemble(doc, h_blocks, h_ref)
    for step in range(INNER):
        pair = split(factor)
        which = [b for b in range(blocks) if step or b not in begun]
        total = begun_ref[...] if begun and not step else None
        total = numerator([m_refs[b] for b in which], rows, weights, which, pair, total)
        factor = factor * total / weights[4][...]
    h_ref[...] = factor
    for b in range(blocks):
        back_refs[b][...] = h_ref[pl.ds(pl.multiple_of((doc ^ b) * share, 8), share), :]
    pair = split(factor)
    ones = jnp.ones((PAD, width), jnp.bfloat16)
    row_sum = dot_nt(ones, pair[0]) + dot_nt(ones, pair[1])

    def put(b, half, near, left, right):
        kept, gone = jnp.where(even, left, right), jnp.where(even, right, left)
        for value, out, before in ((kept, kept_out, sums_in[0]), (gone, sent_out, sums_in[1])):
            out[b, half, near, :] = value if first else before[b, half, near, :] + value

    for b in range(blocks):
        high, low = ratio_of(m_refs[b], rows, weights, b, pair)
        term = dot_nt(high, pair[0]) + (dot_nt(high, pair[1]) + dot_nt(low, pair[0]))
        for half in range(parts // 2):
            at = 2 * half * part_rows
            left, right = term[at : at + part_rows, :], term[at + part_rows : at + 2 * part_rows, :]
            put(b, half, slice(0, part_rows), left, right)
            put(b, half, slice(part_rows, part_rows + PAD), row_sum, row_sum)


def update_piece(m_blocks, h_blocks, rows, weights, sums, parts, early):
    blocks = len(m_blocks)
    width = m_blocks[0].shape[1]
    rank = weights[0].shape[1]
    share = rank // blocks
    first = sums is None
    half_shape = jax.ShapeDtypeStruct((blocks, parts // 2, rows // parts + PAD, rank), jnp.float32)
    back_shape = jax.ShapeDtypeStruct((share, width), jnp.float32)
    total_shape = jax.ShapeDtypeStruct((rank, width), jnp.float32)
    extra = {
        "scratch_shapes": [pltpu.VMEM((rank, width), jnp.float32)],
        "compiler_params": pltpu.CompilerParams(vmem_limit_bytes=VMEM),
    }

    def cost(dots):
        return pl.CostEstimate(
            flops=2 * dots * blocks * rows * width * rank,
            bytes_accessed=blocks * rows * (4 * width + 16 * rank),
            transcendentals=0,
        )

    begun = []
    if early:
        begun = [
            pl.pallas_call(
                functools.partial(begin_kernel, blocks, rows, early),
                out_shape=total_shape,
                in_specs=vmem_space(len(early) + blocks + 5),
                out_specs=vmem_space(1)[0],
                cost_estimate=cost(6),
                name="begin_piece",
                **extra,
            )(*[m_blocks[b] for b in early], *h_blocks, *weights)
        ]
    sums = [] if first else list(sums)
    given = [*m_blocks, *h_blocks, *weights, *begun, *sums]
    *backs, kept, sent = pl.pallas_call(
        functools.partial(piece_kernel, blocks, parts, rows, early, first),
        out_shape=[back_shape] * blocks + [half_shape] * 2,
        in_specs=vmem_space(len(given)),
        out_specs=vmem_space(blocks + 2),
        input_output_aliases={} if first else {len(given) - 2 + i: blocks + i for i in range(2)},
        cost_estimate=cost(15),
        name="update_piece",
        **extra,
    )(*given)
    return backs, (kept, sent), begun


def update_plain(m_blocks, h_blocks, rows, whole_w, sums, parts, doc, feat):
    highest = lax.Precision.HIGHEST
    blocks, rank = len(m_blocks), whole_w.shape[1]
    share, width = rank // blocks, m_blocks[0].shape[1]
    whole_m = jnp.concatenate([m[:rows] for m in m_blocks], axis=0)
    factor = jnp.zeros((rank, width), jnp.float32)
    for k in range(blocks):
        factor = lax.dynamic_update_slice(factor, h_blocks[k], ((doc ^ k) * share, 0))
    column = jnp.sum(whole_w, axis=0)[:, None]
    for _ in range(INNER):
        ratio = whole_m / jnp.dot(whole_w, factor, precision=highest)
        numer = lax.dot_general(whole_w, ratio, (((0,), (0,)), ((), ())), precision=highest)
        factor = factor * numer / column
    ratio = whole_m / jnp.dot(whole_w, factor, precision=highest)
    wnumer = lax.dot_general(ratio, factor, NT, precision=highest)
    wnumer = wnumer.reshape(blocks, parts, rows // parts, rank)
    row_sum = jnp.broadcast_to(jnp.sum(factor, axis=1), (blocks, parts, PAD, rank))
    more = jnp.concatenate([wnumer, row_sum], axis=2)
    more = more.reshape(blocks, parts // 2, 2, *more.shape[2:])
    halves = [lax.dynamic_index_in_dim(more, (feat & 1) ^ i, 2, keepdims=False) for i in range(2)]
    if sums is not None:
        halves = [old + new for old, new in zip(sums, halves)]
    backs = [lax.dynamic_slice_in_dim(factor, (doc ^ k) * share, share, 0) for k in range(blocks)]
    return backs, halves, []


def spread_feat(value, bits):
    got = {0: value}
    for j in reversed(range(bits)):
        for mask, held in list(got.items()):
            pairs = xor_pairs(1 << bits, 1 << j)
            got[mask | 1 << j] = lax.ppermute(held, "feat", pairs)
    return [got[mask] for mask in range(1 << bits)]


def in_order(parts, feat):
    rows = parts[0].shape[0]
    whole = jnp.zeros((rows * len(parts), *parts[0].shape[1:]), parts[0].dtype)
    for mask, part in enumerate(parts):
        whole = lax.dynamic_update_slice_in_dim(whole, part, (feat ^ mask) * rows, 0)
    return whole


def add_feat(kept, sent, bits, feat):
    held = [kept, lax.ppermute(sent, "feat", xor_pairs(1 << bits, 1))]
    shape = kept.shape
    held = [h.reshape((shape[0],) + (2,) * (bits - 1) + shape[2:]) for h in held]
    for j in range(1, bits):
        bit = (feat >> j) & 1
        axis = bits - j

        def half(side):
            return sum(lax.dynamic_index_in_dim(h, side, axis, keepdims=False) for h in held)

        other = lax.ppermute(half(1 - bit), "feat", xor_pairs(1 << bits, 1 << j))
        held = [half(bit), other]
    return held


def after(value, earlier):
    return lax.optimization_barrier((value, *earlier))[0] if earlier else value


def piece_widths(owned):
    return [owned] if owned % WIDTH else [WIDTH] * (owned // WIDTH)


def body(n_doc, n_feat, matrix, doc_factor, feat_factor):
    doc, feat = lax.axis_index("doc"), lax.axis_index("feat")
    bits = n_feat.bit_length() - 1
    rows, columns = matrix.shape
    share, rank = feat_factor.shape[0], doc_factor.shape[1]
    owned = columns // n_doc
    widths = piece_widths(owned)
    pieces = len(widths)
    starts = [sum(widths[:p]) for p in range(pieces)]
    part_rows = rows // n_feat
    others = list(range(n_doc - 1, 0, -1))
    in_kernel = n_doc * rows * rank * 32 < VMEM and widths[0] % 128 == 0 and part_rows % 128 == 0
    w_rides = widths[0] == rank

    def send(value, k):
        return lax.ppermute(value, "doc", xor_pairs(n_doc, k)) if k else value

    riders = [[0, 1][:pieces]] + [[p + 1] if p + 1 < pieces else [] for p in range(1, pieces)]
    w_row = rows + share * len(riders[0])

    def m_piece(p, *earlier):
        given = [after(matrix, earlier), feat_factor]
        height = rows + share * len(riders[p])
        w_mask = n_doc // 2 if w_rides and p == 0 else -1
        given += [doc_factor] if w_mask > 0 else []
        got = {}
        far = [k for k in others if k >= n_doc // 2]
        near = [k for k in range(n_doc // 2 - 1, -1, -1)]
        for masks in (far, near) if p == 0 else (far + near,):
            place = (owned, starts[p], [starts[q] for q in riders[p]], widths[p], masks, height)
            place += (w_mask, part_rows)
            arrays = cut(given, *place) if in_kernel else cut_plain(given, doc, feat, *place)
            got |= {k: send(piece, k) for k, piece in zip(masks, arrays)}
            given = [after(given[0], arrays), *given[1:]]
        return [got[k] for k in range(n_doc)]

    m_pieces = []
    for p in range(pieces):
        gate = m_pieces[p - 2][1:] if p > 1 else m_pieces[0][1:2] if p else []
        m_pieces.append(m_piece(p, *gate))

    w_part = lax.dynamic_slice_in_dim(doc_factor, feat * part_rows, part_rows, 0)
    far = n_doc // 2
    got = {0: w_part, far: m_pieces[0][far][w_row:] if w_rides else send(w_part, far)}
    while far > 1:
        far //= 2
        got |= {mask | far: send(held, far) for mask, held in got.items()}
    w_parts = [got[k] for k in range(1, n_doc)]
    w_parts = spread_feat(jnp.concatenate(w_parts, axis=0), bits)
    if in_kernel:
        weights = prepare(doc_factor, w_parts, n_doc)
    else:
        w_parts = [w.reshape(n_doc - 1, part_rows, rank).swapaxes(0, 1) for w in w_parts]
        w_others = in_order(w_parts, feat).swapaxes(0, 1).reshape(-1, rank)
        whole_w = jnp.concatenate([doc_factor, w_others], axis=0)

    sums = None
    backs = []
    for p in range(pieces):
        source = 0 if p < 2 else p - 1
        at = rows + share * (p == 1)
        ready = backs[-1][:1] if backs else []
        h_blocks = [after(m[at : at + share], ready) for m in m_pieces[source]]
        place = (m_pieces[p], h_blocks, rows)
        if in_kernel:
            early = list(range(n_doc - 1)) if p and p == pieces - 1 else []
            rows_back, sums, begun = update_piece(*place, weights, sums, n_feat, early)
        else:
            rows_back, sums, begun = update_plain(*place, whole_w, sums, n_feat, doc, feat)
        backs.append(rows_back)

    def give_back(batch, *earlier):
        rows_of = [jnp.concatenate([b[k] for b in batch], axis=0) for k in range(n_doc)]
        return [send(after(r, earlier), k) for k, r in enumerate(rows_of)]

    batches = [b for b in (backs[:1], backs[1:]) if b]
    returned = [give_back(b, *begun) for b in batches[:-1]]
    kept, sent = sums
    kept, other = add_feat(kept, after(sent, [r for got in returned for r in got[1:]]), bits, feat)
    returned.append(give_back(batches[-1]))
    kept = after(kept, returned[-1][1:])
    total = kept[0] + other[0]
    for k in range(1, n_doc):
        total = total + send(kept[k] + other[k], k)
    new_part = w_part * total[:part_rows] / total[part_rows]
    new_parts = spread_feat(new_part, bits)
    new_doc = in_order(new_parts, feat)
    new_feat = jnp.zeros((share, columns), jnp.float32)
    start = 0
    for batch, rows_of in zip(batches, returned):
        for k, value in enumerate(rows_of):
            value = value.reshape(len(batch), share, -1).swapaxes(0, 1).reshape(share, -1)
            value = after(value, new_parts[-1:])
            new_feat = lax.dynamic_update_slice(new_feat, value, (0, (doc ^ k) * owned + start))
        start += value.shape[1]
    return new_doc, new_feat


def solution(mesh):
    placed = (P(("grp", "doc"), "feat"), P(("grp", "doc"), None), P(("grp", "doc"), "feat"))
    return jax.shard_map(
        functools.partial(body, mesh.shape["doc"], mesh.shape["feat"]),
        mesh=mesh,
        in_specs=placed,
        out_specs=(P(("grp", "doc"), None), P(("grp", "doc"), "feat")),
        check_vma=False,
    )
```

```python
import functools

import jax
import jax.numpy as jnp
from jax import lax
from jax.experimental import pallas as pl
from jax.experimental.pallas import tpu as pltpu
from jax.sharding import PartitionSpec as P

INNER = 2
WIDTH = 256
PAD = 8
VMEM = 17 * 1024 * 1024
NT = (((1,), (1,)), ((), ()))


def xor_pairs(count, mask):
    return [(i, i ^ mask) for i in range(count)]


def split(value):
    high = value.astype(jnp.bfloat16)
    low = (value - high.astype(jnp.float32)).astype(jnp.bfloat16)
    return high, low


def dot(left, right):
    return jnp.dot(left, right, preferred_element_type=jnp.float32)


def dot3(left, right):
    return dot(left[0], right[0]) + (dot(left[0], right[1]) + dot(left[1], right[0]))


def dot_nt(left, right):
    return lax.dot_general(left, right, NT, preferred_element_type=jnp.float32)


def any_space(count):
    return [pl.BlockSpec(memory_space=pl.ANY)] * count


def vmem_space(count):
    return [pl.BlockSpec(memory_space=pltpu.VMEM)] * count


def cut_kernel(spec, *refs):
    owned, start, h_starts, width, masks, sources, w_mask = spec
    given, outs, sems = refs[:sources], refs[sources:-1], refs[-1]
    doc, feat = lax.axis_index("doc"), lax.axis_index("feat")
    copies = []
    for mask, out in zip(masks, outs):
        row = 0
        for ref, first in [(given[0], start)] + [(given[1], first) for first in h_starts]:
            rows = ref.shape[0]
            begin = pl.multiple_of((doc ^ mask) * owned + first, 128)
            copies.append((ref.at[:, pl.ds(begin, width)], out.at[pl.ds(row, rows), :]))
            row += rows
        if mask == w_mask:
            rows = out.shape[0] - row
            near = pl.multiple_of(feat * rows, 8)
            copies.append((given[2].at[pl.ds(near, rows), :], out.at[pl.ds(row, rows), :]))
    copies = [pltpu.make_async_copy(*pair, sems.at[i]) for i, pair in enumerate(copies)]
    for copy in copies:
        copy.start()
    for copy in copies:
        copy.wait()


def cut(given, owned, start, h_starts, width, masks, rows, w_mask, w_rows):
    spec = (owned, start, tuple(h_starts), width, tuple(masks), len(given), w_mask)
    count = (1 + len(h_starts)) * len(masks) + 1
    heights = [rows + w_rows * (mask == w_mask) for mask in masks]
    return pl.pallas_call(
        functools.partial(cut_kernel, spec),
        out_shape=[jax.ShapeDtypeStruct((height, width), jnp.float32) for height in heights],
        in_specs=any_space(len(given)),
        out_specs=vmem_space(len(masks)),
        scratch_shapes=[pltpu.SemaphoreType.DMA((count,))],
        cost_estimate=pl.CostEstimate(
            flops=0, bytes_accessed=8 * rows * width * len(masks), transcendentals=0
        ),
        name="cut_piece",
    )(*given)


def cut_plain(given, doc, feat, owned, start, h_starts, width, masks, rows, w_mask, w_rows):
    outs = []
    for mask in masks:
        begin = (doc ^ mask) * owned
        sources = [(given[0], start)] + [(given[1], first) for first in h_starts]
        parts = [lax.dynamic_slice(g, (0, begin + f), (g.shape[0], width)) for g, f in sources]
        if mask == w_mask:
            parts.append(lax.dynamic_slice_in_dim(given[2], feat * w_rows, w_rows, 0))
        outs.append(jnp.concatenate(parts, axis=0))
    return outs


def prepare_kernel(blocks, own_ref, *refs):
    part_refs, (high_ref, low_ref, high_t_ref, low_t_ref, sum_ref) = refs[:-5], refs[-5:]
    feat = lax.axis_index("feat")
    rows = own_ref.shape[0]
    part_rows = rows // len(part_refs)

    def place(value, row, count):
        near = pl.ds(row, count)
        high_ref[near, :], low_ref[near, :] = split(value)
        turned = value.T
        high_t_ref[:, near], low_t_ref[:, near] = split(turned)
        return jnp.sum(turned, axis=1, keepdims=True)

    total = place(own_ref[...], 0, rows)
    for mask, ref in enumerate(part_refs):
        at = (feat ^ mask) * part_rows
        for b in range(1, blocks):
            value = ref[(b - 1) * part_rows : b * part_rows, :]
            total = total + place(value, pl.multiple_of(b * rows + at, 128), part_rows)
    sum_ref[...] = total


def prepare(own, parts, blocks):
    rows, rank = own.shape
    docs = blocks * rows
    half = jnp.bfloat16
    shapes = [
        jax.ShapeDtypeStruct((docs, rank), half),
        jax.ShapeDtypeStruct((docs, rank), half),
        jax.ShapeDtypeStruct((rank, docs), half),
        jax.ShapeDtypeStruct((rank, docs), half),
        jax.ShapeDtypeStruct((rank, 1), jnp.float32),
    ]
    return pl.pallas_call(
        functools.partial(prepare_kernel, blocks),
        out_shape=shapes,
        in_specs=vmem_space(1 + len(parts)),
        out_specs=vmem_space(len(shapes)),
        compiler_params=pltpu.CompilerParams(vmem_limit_bytes=VMEM),
        cost_estimate=pl.CostEstimate(flops=0, bytes_accessed=docs * rank * 12, transcendentals=0),
        name="prepare_w",
    )(own, *parts)


def assemble(doc, h_blocks, h_ref):
    share = h_blocks[0].shape[0]
    for b, block in enumerate(h_blocks):
        h_ref[pl.ds(pl.multiple_of((doc ^ b) * share, 8), share), :] = block[...]
    return h_ref[...]


def ratio_of(m_ref, rows, weights, b, pair):
    near = slice(b * rows, (b + 1) * rows)
    return split(m_ref[:rows, :] / dot3((weights[0][near, :], weights[1][near, :]), pair))


def numerator(m_refs, rows, weights, which, pair, total):
    for m_ref, b in zip(m_refs, which):
        near = slice(b * rows, (b + 1) * rows)
        turned = (weights[2][:, near], weights[3][:, near])
        term = dot3(turned, ratio_of(m_ref, rows, weights, b, pair))
        total = term if total is None else total + term
    return total


def begin_kernel(blocks, rows, which, *refs):
    count = len(which)
    m_refs, h_blocks = refs[:count], refs[count : count + blocks]
    weights, total_ref, h_ref = refs[count + blocks : -2], refs[-2], refs[-1]
    factor = assemble(lax.axis_index("doc"), h_blocks, h_ref)
    total_ref[...] = numerator(m_refs, rows, weights, which, split(factor), None)


def piece_kernel(blocks, parts, rows, begun, first, *refs):
    m_refs, h_blocks = refs[:blocks], refs[blocks : 2 * blocks]
    weights, rest = refs[2 * blocks : 2 * blocks + 5], list(refs[2 * blocks + 5 :])
    begun_ref = rest.pop(0) if begun else None
    sums_in = (None, None) if first else (rest.pop(0), rest.pop(0))
    *back_refs, kept_out, sent_out, h_ref = rest
    width = h_ref.shape[1]
    share = h_blocks[0].shape[0]
    part_rows = rows // parts
    doc, feat = lax.axis_index("doc"), lax.axis_index("feat")
    even = (feat & 1) == 0

    factor = assemble(doc, h_blocks, h_ref)
    for step in range(INNER):
        pair = split(factor)
        which = [b for b in range(blocks) if step or b not in begun]
        total = begun_ref[...] if begun and not step else None
        total = numerator([m_refs[b] for b in which], rows, weights, which, pair, total)
        factor = factor * total / weights[4][...]
    h_ref[...] = factor
    for b in range(blocks):
        back_refs[b][...] = h_ref[pl.ds(pl.multiple_of((doc ^ b) * share, 8), share), :]
    pair = split(factor)
    ones = jnp.ones((PAD, width), jnp.bfloat16)
    row_sum = dot_nt(ones, pair[0]) + dot_nt(ones, pair[1])

    def put(b, half, near, left, right):
        kept, gone = jnp.where(even, left, right), jnp.where(even, right, left)
        for value, out, before in ((kept, kept_out, sums_in[0]), (gone, sent_out, sums_in[1])):
            out[b, half, near, :] = value if first else before[b, half, near, :] + value

    for b in range(blocks):
        high, low = ratio_of(m_refs[b], rows, weights, b, pair)
        term = dot_nt(high, pair[0]) + (dot_nt(high, pair[1]) + dot_nt(low, pair[0]))
        for half in range(parts // 2):
            at = 2 * half * part_rows
            left, right = term[at : at + part_rows, :], term[at + part_rows : at + 2 * part_rows, :]
            put(b, half, slice(0, part_rows), left, right)
            put(b, half, slice(part_rows, part_rows + PAD), row_sum, row_sum)


def update_piece(m_blocks, h_blocks, rows, weights, sums, parts, early):
    blocks = len(m_blocks)
    width = m_blocks[0].shape[1]
    rank = weights[0].shape[1]
    share = rank // blocks
    first = sums is None
    half_shape = jax.ShapeDtypeStruct((blocks, parts // 2, rows // parts + PAD, rank), jnp.float32)
    back_shape = jax.ShapeDtypeStruct((share, width), jnp.float32)
    total_shape = jax.ShapeDtypeStruct((rank, width), jnp.float32)
    extra = {
        "scratch_shapes": [pltpu.VMEM((rank, width), jnp.float32)],
        "compiler_params": pltpu.CompilerParams(vmem_limit_bytes=VMEM),
    }

    def cost(dots):
        return pl.CostEstimate(
            flops=2 * dots * blocks * rows * width * rank,
            bytes_accessed=blocks * rows * (4 * width + 16 * rank),
            transcendentals=0,
        )

    begun = []
    if early:
        begun = [
            pl.pallas_call(
                functools.partial(begin_kernel, blocks, rows, early),
                out_shape=total_shape,
                in_specs=vmem_space(len(early) + blocks + 5),
                out_specs=vmem_space(1)[0],
                cost_estimate=cost(6),
                name="begin_piece",
                **extra,
            )(*[m_blocks[b] for b in early], *h_blocks, *weights)
        ]
    sums = [] if first else list(sums)
    given = [*m_blocks, *h_blocks, *weights, *begun, *sums]
    *backs, kept, sent = pl.pallas_call(
        functools.partial(piece_kernel, blocks, parts, rows, early, first),
        out_shape=[back_shape] * blocks + [half_shape] * 2,
        in_specs=vmem_space(len(given)),
        out_specs=vmem_space(blocks + 2),
        input_output_aliases={} if first else {len(given) - 2 + i: blocks + i for i in range(2)},
        cost_estimate=cost(15),
        name="update_piece",
        **extra,
    )(*given)
    return backs, (kept, sent), begun


def update_plain(m_blocks, h_blocks, rows, whole_w, sums, parts, doc, feat):
    highest = lax.Precision.HIGHEST
    blocks, rank = len(m_blocks), whole_w.shape[1]
    share, width = rank // blocks, m_blocks[0].shape[1]
    whole_m = jnp.concatenate([m[:rows] for m in m_blocks], axis=0)
    factor = jnp.zeros((rank, width), jnp.float32)
    for k in range(blocks):
        factor = lax.dynamic_update_slice(factor, h_blocks[k], ((doc ^ k) * share, 0))
    column = jnp.sum(whole_w, axis=0)[:, None]
    for _ in range(INNER):
        ratio = whole_m / jnp.dot(whole_w, factor, precision=highest)
        numer = lax.dot_general(whole_w, ratio, (((0,), (0,)), ((), ())), precision=highest)
        factor = factor * numer / column
    ratio = whole_m / jnp.dot(whole_w, factor, precision=highest)
    wnumer = lax.dot_general(ratio, factor, NT, precision=highest)
    wnumer = wnumer.reshape(blocks, parts, rows // parts, rank)
    row_sum = jnp.broadcast_to(jnp.sum(factor, axis=1), (blocks, parts, PAD, rank))
    more = jnp.concatenate([wnumer, row_sum], axis=2)
    more = more.reshape(blocks, parts // 2, 2, *more.shape[2:])
    halves = [lax.dynamic_index_in_dim(more, (feat & 1) ^ i, 2, keepdims=False) for i in range(2)]
    if sums is not None:
        halves = [old + new for old, new in zip(sums, halves)]
    backs = [lax.dynamic_slice_in_dim(factor, (doc ^ k) * share, share, 0) for k in range(blocks)]
    return backs, halves, []


def spread_feat(value, bits):
    got = {0: value}
    for j in reversed(range(bits)):
        for mask, held in list(got.items()):
            pairs = xor_pairs(1 << bits, 1 << j)
            got[mask | 1 << j] = lax.ppermute(held, "feat", pairs)
    return [got[mask] for mask in range(1 << bits)]


def in_order(parts, feat):
    rows = parts[0].shape[0]
    whole = jnp.zeros((rows * len(parts), *parts[0].shape[1:]), parts[0].dtype)
    for mask, part in enumerate(parts):
        whole = lax.dynamic_update_slice_in_dim(whole, part, (feat ^ mask) * rows, 0)
    return whole


def add_feat(kept, sent, bits, feat):
    held = [kept, lax.ppermute(sent, "feat", xor_pairs(1 << bits, 1))]
    shape = kept.shape
    held = [h.reshape((shape[0],) + (2,) * (bits - 1) + shape[2:]) for h in held]
    for j in range(1, bits):
        bit = (feat >> j) & 1
        axis = bits - j

        def half(side):
            return sum(lax.dynamic_index_in_dim(h, side, axis, keepdims=False) for h in held)

        other = lax.ppermute(half(1 - bit), "feat", xor_pairs(1 << bits, 1 << j))
        held = [half(bit), other]
    return held


def after(value, earlier):
    return lax.optimization_barrier((value, *earlier))[0] if earlier else value


def piece_widths(owned):
    return [owned] if owned % WIDTH else [WIDTH] * (owned // WIDTH)


def body(n_doc, n_feat, matrix, doc_factor, feat_factor):
    doc, feat = lax.axis_index("doc"), lax.axis_index("feat")
    bits = n_feat.bit_length() - 1
    rows, columns = matrix.shape
    share, rank = feat_factor.shape[0], doc_factor.shape[1]
    owned = columns // n_doc
    widths = piece_widths(owned)
    pieces = len(widths)
    starts = [sum(widths[:p]) for p in range(pieces)]
    part_rows = rows // n_feat
    others = list(range(n_doc - 1, 0, -1))
    in_kernel = n_doc * rows * rank * 32 < VMEM and widths[0] % 128 == 0 and part_rows % 128 == 0
    w_rides = widths[0] == rank

    def send(value, k):
        return lax.ppermute(value, "doc", xor_pairs(n_doc, k)) if k else value

    riders = [[0, 1][:pieces]] + [[p + 1] if p + 1 < pieces else [] for p in range(1, pieces)]
    w_row = rows + share * len(riders[0])

    def m_piece(p, *earlier):
        given = [after(matrix, earlier), feat_factor]
        height = rows + share * len(riders[p])
        w_mask = n_doc // 2 if w_rides and p == 0 else -1
        given += [doc_factor] if w_mask > 0 else []
        got = {}
        far = [k for k in others if k >= n_doc // 2]
        near = [k for k in range(n_doc // 2 - 1, -1, -1)]
        for masks in (far, near) if p == 0 else (far + near,):
            place = (owned, starts[p], [starts[q] for q in riders[p]], widths[p], masks, height)
            place += (w_mask, part_rows)
            arrays = cut(given, *place) if in_kernel else cut_plain(given, doc, feat, *place)
            got |= {k: send(piece, k) for k, piece in zip(masks, arrays)}
            given = [after(given[0], arrays), *given[1:]]
        return [got[k] for k in range(n_doc)]

    m_pieces = []
    for p in range(pieces):
        gate = m_pieces[p - 2][1:] if p > 1 else m_pieces[0][1:2] if p else []
        m_pieces.append(m_piece(p, *gate))

    w_part = lax.dynamic_slice_in_dim(doc_factor, feat * part_rows, part_rows, 0)
    far = n_doc // 2
    got = {0: w_part, far: m_pieces[0][far][w_row:] if w_rides else send(w_part, far)}
    while far > 1:
        far //= 2
        got |= {mask | far: send(held, far) for mask, held in got.items()}
    w_parts = [got[k] for k in range(1, n_doc)]
    w_parts = spread_feat(jnp.concatenate(w_parts, axis=0), bits)
    if in_kernel:
        weights = prepare(doc_factor, w_parts, n_doc)
    else:
        w_parts = [w.reshape(n_doc - 1, part_rows, rank).swapaxes(0, 1) for w in w_parts]
        w_others = in_order(w_parts, feat).swapaxes(0, 1).reshape(-1, rank)
        whole_w = jnp.concatenate([doc_factor, w_others], axis=0)

    sums = None
    backs = []
    for p in range(pieces):
        source = 0 if p < 2 else p - 1
        at = rows + share * (p == 1)
        ready = backs[-1][:1] if backs else []
        h_blocks = [after(m[at : at + share], ready) for m in m_pieces[source]]
        place = (m_pieces[p], h_blocks, rows)
        if in_kernel:
            early = list(range(n_doc - 1)) if p and p == pieces - 1 else []
            rows_back, sums, begun = update_piece(*place, weights, sums, n_feat, early)
        else:
            rows_back, sums, begun = update_plain(*place, whole_w, sums, n_feat, doc, feat)
        backs.append(rows_back)

    def give_back(batch, *earlier):
        rows_of = [jnp.concatenate([b[k] for b in batch], axis=0) for k in range(n_doc)]
        return [send(after(r, earlier), k) for k, r in enumerate(rows_of)]

    batches = [b for b in (backs[:1], backs[1:]) if b]
    returned = [give_back(b, *begun) for b in batches[:-1]]
    kept, sent = sums
    kept, other = add_feat(kept, after(sent, [r for got in returned for r in got[1:]]), bits, feat)
    returned.append(give_back(batches[-1]))
    kept = after(kept, returned[-1][1:])
    total = kept[0] + other[0]
    for k in range(1, n_doc):
        total = total + send(kept[k] + other[k], k)
    new_part = w_part * total[:part_rows] / total[part_rows]
    new_parts = spread_feat(new_part, bits)
    new_doc = in_order(new_parts, feat)
    new_feat = jnp.zeros((share, columns), jnp.float32)
    start = 0
    for batch, rows_of in zip(batches, returned):
        for k, value in enumerate(rows_of):
            value = value.reshape(len(batch), share, -1).swapaxes(0, 1).reshape(share, -1)
            value = after(value, new_parts[-1:])
            new_feat = lax.dynamic_update_slice(new_feat, value, (0, (doc ^ k) * owned + start))
        start += value.shape[1]
    return new_doc, new_feat


def solution(mesh):
    placed = (P(("grp", "doc"), "feat"), P(("grp", "doc"), None), P(("grp", "doc"), "feat"))
    return jax.shard_map(
        functools.partial(body, mesh.shape["doc"], mesh.shape["feat"]),
        mesh=mesh,
        in_specs=placed,
        out_specs=(P(("grp", "doc"), None), P(("grp", "doc"), "feat")),
        check_vma=False,
    )
```
